256 devices in a mesh: cls: 4 (over x), img: 64 (over z, y, core).
Axes of the slice: x: 4, y: 4, z: 8, core: 2. Of those that a mesh axis runs over, the one named last changes fastest.
Arguments:
- particles: bfloat16 [30720, 10000], P('img'), may hold values from -60 to 60
- defocus: float32 [30720], P('img'), may hold values from 0.5 to 3
- freq_sq: float32 [5000], replicated, may hold values from 0.5 to 40
- projections: bfloat16 [64, 384, 10000], P('cls', 'img'), may hold values from -1.5 to 1.5
- priors: int32 [30720, 2], P('img'), may hold values from 0 to 18, as said below
Outputs:
- data_sum: float32 [64, 384, 10000], P('cls', 'img')
- weight_sum: float32 [64, 384, 5000], P('cls', 'img')
- evidence: float32 [30720], P('img')
The draws below stay inside these ranges and needn't reach their ends.
Inputs may be any that keep to these rules, and one draw needn't show every extreme that they name: priors[i, 0] < priors[i, 1]. For each block of 480 particles there is an r of 1 to 3 such that all windows of the block lie in [0, r * 6), and the block's first particle has the window [0, r * 6).
All inputs are finite; a program needn't handle non-finite values.
Results may differ from the reference program's by a relative error of at most 0.0059.
Values may be sent and summed in bfloat16 or wider, within the bound.
A program may use at most 128 MiB of HBM per device.

```python
import math
import jax
import jax.numpy as jnp
from jax import lax

COMP = 5000
F = 10000
CLASSES = 64
ORI_DEV = 6
ORIENT = 384
PART_DEV = 480
PARTICLES = 30720
SPAN = 3


AMPLITUDE_SCALE = 2.5


LOW_FREQ = 0.5


HIGH_FREQ = 40.0


ENVELOPE_CAP = 6.0


def frequency_grid(key):
    key = jax.random.fold_in(key, 13)
    return jax.random.uniform(key, (COMP,), jnp.float32, LOW_FREQ, HIGH_FREQ)


def projection_parts(key, steepest):
    freq = frequency_grid(key)
    key = jax.random.fold_in(key, 11)
    key_normal, key_spread, key_decay = jax.random.split(key, 3)
    normal_part = jnp.clip(jax.random.normal(key_normal, (CLASSES, ORIENT, F), jnp.float32), -5.0, 5.0)
    spread = jnp.exp(jax.random.uniform(key_spread, (CLASSES, ORIENT, 1), jnp.float32, math.log(0.5), math.log(2.0)))
    decay = jnp.exp(jax.random.uniform(key_decay, (CLASSES, ORIENT, 1), jnp.float32, math.log(0.03), math.log(steepest)))
    average = (jnp.exp(-decay * LOW_FREQ) - jnp.exp(-decay * HIGH_FREQ)) / ((HIGH_FREQ - LOW_FREQ) * decay)
    envelope = jnp.minimum(jnp.exp(-0.5 * decay * freq[None, None, :]) / jnp.sqrt(average), ENVELOPE_CAP)
    envelope = jnp.concatenate([envelope, envelope], axis=2)
    amplitude = AMPLITUDE_SCALE * spread
    return (normal_part * envelope * (amplitude / math.sqrt(F)), amplitude * amplitude)


def draw_freq_sq(key, part):
    shared = frequency_grid(key)
    return shared


def draw_projections(key, part):
    steepest = 0.6
    shared = projection_parts(key, steepest)
    return shared[0].astype(jnp.bfloat16)


def draw_particles(key, part):
    key = jax.random.fold_in(key, 5)
    background = jnp.clip(jax.random.normal(key, (PARTICLES, F), jnp.float32), -6.0, 6.0)
    return background.astype(jnp.bfloat16)


def draw_priors(key, part):
    key = jax.random.fold_in(key, 7)
    key_reach, key_lower, key_spans = jax.random.split(key, 3)
    block_count = PARTICLES // PART_DEV
    block_ids = jnp.arange(block_count)
    drawn = jax.random.randint(key_reach, (block_count,), 1, SPAN + 1)
    edge = (block_ids < SPAN) | (block_ids >= block_count - SPAN)
    reaches = jnp.where(edge, SPAN, drawn)
    limits = jnp.repeat(reaches, PART_DEV, total_repeat_length=PARTICLES) * ORI_DEV
    lower = jax.random.randint(key_lower, (PARTICLES,), 0, limits)
    spans = jax.random.randint(key_spans, (PARTICLES,), 1, limits - lower + 1)
    leading = jnp.arange(PARTICLES) % PART_DEV == 0
    upper = jnp.where(leading, limits, lower + spans)
    lower = jnp.where(leading, 0, lower)
    return jnp.stack([lower, upper], axis=1).astype(jnp.int32)


def levels(rng, extent, cuts, least, high):
    level = 1.0
    for dim, shards_of in cuts:
        heights = jax.random.uniform(jax.random.fold_in(jax.random.fold_in(rng, 6), dim), (shards_of,), jnp.float32, least / len(cuts), high / len(cuts))
        level = level * jnp.repeat(jnp.exp(heights), extent[dim] // shards_of).reshape((-1,) + (1,) * (len(extent) - 1 - dim))
    return level


def setup_inputs(seed: int = 0) -> dict:
    seeds = jax.random.split(jax.random.key(seed), 6)
    return {
        "particles": draw_particles(jax.random.fold_in(seeds[5], 71), 0),
        "defocus": jnp.clip(jnp.exp(math.log(3.0) - 1.7917595 * jax.random.uniform(seeds[1], (PARTICLES,), jnp.float32) ** levels(seeds[1], (PARTICLES,), ((0, 64),), -0.2, 0.2)), 0.5, 3.0),
        "freq_sq": draw_freq_sq(jax.random.fold_in(seeds[5], 71), 0),
        "projections": draw_projections(jax.random.fold_in(seeds[5], 71), 0),
        "priors": draw_priors(jax.random.fold_in(seeds[5], 71), 0),
    }


SINE_WEIGHT = 0.99498744
AMPLITUDE = 0.1


def ctf_terms(particles, defocus, freq_sq):
    phase_arg = defocus[:, None] * freq_sq[None, :]
    ctf_abs = jnp.abs(SINE_WEIGHT * jnp.sin(phase_arg) + AMPLITUDE * jnp.cos(phase_arg))
    ctf_sq = (ctf_abs * ctf_abs).astype(jnp.bfloat16)
    weighted = (particles.astype(jnp.float32) * jnp.concatenate([ctf_abs, ctf_abs], axis=1)).astype(jnp.bfloat16)
    return weighted, ctf_sq


def spectrum_of(portion):
    values = portion.astype(jnp.float32)
    half_count = values.shape[-1] // 2
    real_part = values[..., :half_count]
    imag_part = values[..., half_count:]
    return (real_part * real_part + imag_part * imag_part).astype(jnp.bfloat16)


def window_mask(priors, offset, orient_count):
    orient = offset * orient_count + jnp.arange(orient_count, dtype=jnp.int32)
    return (orient[None, :] >= priors[:, 0:1]) & (orient[None, :] < priors[:, 1:2])


def reference(particles, defocus, freq_sq, projections, priors):
    block_count = PARTICLES // PART_DEV

    def one_block(sums_carry, index):
        data_sum, weight_sum = sums_carry
        anchor = index * PART_DEV
        block_particles = lax.dynamic_slice_in_dim(particles, anchor, PART_DEV, 0)
        block_defocus = lax.dynamic_slice_in_dim(defocus, anchor, PART_DEV, 0)
        block_priors = lax.dynamic_slice_in_dim(priors, anchor, PART_DEV, 0)
        weighted, ctf_sq = ctf_terms(block_particles, block_defocus, freq_sq)
        weighted_full = lax.optimization_barrier(weighted).astype(jnp.float32)
        ctf_sq_full = lax.optimization_barrier(ctf_sq).astype(jnp.float32)
        logit_list = []
        places = []
        for offset in range(SPAN):
            place = ((index + offset) % block_count) * ORI_DEV
            portion = lax.dynamic_slice_in_dim(projections, place, ORI_DEV, 1)
            spectrum = lax.optimization_barrier(spectrum_of(portion)).astype(jnp.float32)
            crossed = jnp.einsum("pf,cof->pco", weighted_full, portion.astype(jnp.float32))
            damping = jnp.einsum("pm,com->pco", ctf_sq_full, spectrum)
            allowed = window_mask(block_priors, offset, ORI_DEV)
            logit_list.append(jnp.where(allowed[:, None, :], crossed - 0.5 * damping, -jnp.inf))
            places.append(place)
        logits = jnp.stack(logit_list, axis=1)
        highest = jnp.max(logits, axis=(1, 2, 3))
        scaled = jnp.exp(logits - highest[:, None, None, None])
        totals = jnp.sum(scaled, axis=(1, 2, 3))
        evidence = highest + jnp.log(totals)
        posterior = (scaled / totals[:, None, None, None]).astype(jnp.bfloat16)
        posterior = lax.optimization_barrier(posterior).astype(jnp.float32)
        for offset in range(SPAN):
            data_part = jnp.einsum("pco,pf->cof", posterior[:, offset], weighted_full)
            weight_part = jnp.einsum("pco,pm->com", posterior[:, offset], ctf_sq_full)
            old_data = lax.dynamic_slice_in_dim(data_sum, places[offset], ORI_DEV, 1)
            data_sum = lax.dynamic_update_slice_in_dim(data_sum, old_data + data_part, places[offset], 1)
            old_weight = lax.dynamic_slice_in_dim(weight_sum, places[offset], ORI_DEV, 1)
            weight_sum = lax.dynamic_update_slice_in_dim(weight_sum, old_weight + weight_part, places[offset], 1)
        return (data_sum, weight_sum), evidence

    initial = (jnp.zeros((CLASSES, ORIENT, F), jnp.float32), jnp.zeros((CLASSES, ORIENT, COMP), jnp.float32))
    sums_final, evidence = lax.scan(one_block, initial, jnp.arange(block_count, dtype=jnp.int32))
    return sums_final[0], sums_final[1], evidence.reshape(PARTICLES)
```

```python
import functools
import math

import jax
import jax.numpy as jnp
import numpy as np
from jax import lax
from jax.experimental import pallas as pl
from jax.experimental.pallas import tpu as pltpu
from jax.sharding import PartitionSpec as P

SPAN = 3
SINE_WEIGHT = 0.99498744
AMPLITUDE = 0.1
MESH = pl.DeviceIdType.MESH

CHUNK = 1280
GROUP = 16
SLOTS = 4


def sine_series(terms):
    r = np.cos(np.linspace(0.0, np.pi, 4001)) * 0.5
    powers = np.stack([r ** (2 * i + 1) for i in range(terms)], axis=1)
    return np.linalg.lstsq(powers, np.sin(np.pi * r), rcond=None)[0]


SERIES = [float(v) * math.hypot(SINE_WEIGHT, AMPLITUDE) for v in sine_series(4)]
PHASE = math.atan2(AMPLITUDE, SINE_WEIGHT) / math.pi
ROUNDER = 12582912.0


def ctf_of(defocus, freq):
    turns = defocus * freq + jnp.float32(PHASE)
    whole = (turns + jnp.float32(ROUNDER)) - jnp.float32(ROUNDER)
    rest = turns - whole
    square = rest * rest
    series = jnp.float32(SERIES[3])
    for term in SERIES[2::-1]:
        series = series * square + jnp.float32(term)
    return jnp.abs(series * rest)


def kernel(
    n_img, cls_n, classes,
    particles_ref, defocus_ref, freq_ref, proj_ref, priors_ref,
    data_ref, weight_ref, evidence_ref,
    stage, proj_stage, proj, weighted, ctf_sq, freq, d_row, d_recv, d_col,
    scores, logits, post, post_recv, window, top_send, top_recv,
    near, sib_recv, far, far_send, own, far_recv, ctf_next,
    stage_sem, proj_sem, d_send_sem, d_recv_sem,
    ici_send_sem, ici_recv_sem, sib_send_sem, sib_recv_sem,
    top_send_sem, top_recv_sem, post_send_sem, post_recv_sem,
    sum_send_sem, sum_recv_sem, part_send_sem, part_recv_sem,
):
    count, real = particles_ref.shape
    comp = real // 2
    rows = proj_ref.shape[0]
    pad_real = proj.shape[2]
    pad_count = weighted.shape[0]
    chunks = pad_real // CHUNK
    last = (chunks - 1) * CHUNK
    groups = count // GROUP

    f32, bf16 = jnp.float32, jnp.bfloat16

    c, i = lax.axis_index("cls"), lax.axis_index("img")
    core = lax.rem(i, 2)
    sib = i + 1 - 2 * core
    up1, up2 = lax.rem(i + 1, n_img), lax.rem(i + 2, n_img)
    dn1, dn2 = lax.rem(i + n_img - 1, n_img), lax.rem(i + n_img - 2, n_img)
    others = [lax.rem(c + step, cls_n) for step in range(1, cls_n)]

    def span(k):
        return pl.ds(pl.multiple_of(k * CHUNK, CHUNK), CHUNK)

    def send(src, dst, send_sem, recv_sem, img, cls=c):
        return pltpu.make_async_remote_copy(
            src_ref=src, dst_ref=dst, send_sem=send_sem, recv_sem=recv_sem,
            device_id=(cls, img), device_id_type=MESH,
        )

    def fetch(g):
        slot = lax.rem(g, SLOTS)
        return pltpu.make_async_copy(
            particles_ref.at[pl.ds(pl.multiple_of(g * GROUP, GROUP), GROUP), :],
            stage.at[slot], stage_sem.at[slot],
        )

    proj_copy = pltpu.make_async_copy(proj_ref, proj_stage, proj_sem)
    proj_copy.start()
    for g in range(SLOTS):
        fetch(g).start()

    barrier = pltpu.get_barrier_semaphore()
    for img in (sib, up2, dn2, dn1):
        pl.semaphore_signal(barrier, inc=1, device_id=(c, img), device_id_type=MESH)
    for cls in others:
        pl.semaphore_signal(barrier, inc=1, device_id=(cls, i), device_id_type=MESH)

    d_row[...] = jnp.zeros_like(d_row)
    d_row[0:1, 0:count] = defocus_ref[...]
    freq[...] = jnp.zeros_like(freq)
    over_pi = freq_ref[...] * f32(1.0 / math.pi)
    freq[0:1, 0:comp] = over_pi
    freq[0:1, comp:real] = over_pi
    window[0:1, :] = jnp.zeros((1, pad_count), jnp.int32)
    window[1:2, :] = jnp.full((1, pad_count), SPAN * rows, jnp.int32)
    window[0:2, 0:count] = priors_ref[...]
    weighted[count:, :] = jnp.zeros((pad_count - count, pad_real), bf16)
    ctf_sq[count:, :] = jnp.zeros((pad_count - count, pad_real), bf16)
    ctf_next[:, count:, :] = jnp.zeros((2, pad_count - count, CHUNK), bf16)
    scores[...] = jnp.zeros_like(scores)
    edge = real // 128 * 128
    proj[0, :, edge:] = jnp.zeros((rows, pad_real - edge), bf16)
    weighted[0:count, edge:] = jnp.zeros((count, pad_real - edge), bf16)

    pl.semaphore_wait(barrier, 4 + len(others))

    def direct(k):
        return send(
            proj.at[0, :, span(k)], proj.at[2, :, span(k)],
            ici_send_sem.at[k], ici_recv_sem.at[k], dn2,
        )

    proj_copy.wait()
    for k in range(chunks):
        lo, hi = k * CHUNK, min((k + 1) * CHUNK, real)
        proj[0, :, lo:hi] = proj_stage[:, lo:hi]
        direct(k).start()
    d_copies = [
        send(d_row, d_recv.at[n], d_send_sem.at[n], d_recv_sem.at[n], img)
        for n, img in enumerate((up1, up2))
    ]
    for copy in d_copies:
        copy.start()

    def column(row):
        return jnp.transpose(jnp.broadcast_to(row, (128, pad_count)))

    d_col[0] = column(d_row[0:1, :])

    tile = 2 * CHUNK

    def weigh(g, carry):
        fetch(g).wait()
        slot = lax.rem(g, SLOTS)
        at = pl.ds(pl.multiple_of(g * GROUP, GROUP), GROUP)
        defocus = d_col[0, at, 0:1]
        for lo in range(0, pad_real, tile):
            width = min(tile, real - lo)
            ctf = ctf_of(defocus, freq[0:1, lo : lo + tile])
            ctf_sq[at, lo : lo + tile] = (ctf * ctf).astype(bf16)
            image = stage[slot, :, lo : lo + width].astype(f32)
            weighted[at, lo : lo + width] = (image * ctf[:, :width]).astype(bf16)

        @pl.when(g + SLOTS < groups)
        def _():
            fetch(g + SLOTS).start()

        return carry

    lax.fori_loop(0, groups, weigh, 0)

    shared = 2 * (1 - core)

    def relay(k):
        return send(
            proj.at[shared, :, span(k)], proj.at[1, :, span(k)],
            sib_send_sem.at[k], sib_recv_sem.at[k], sib,
        )

    contract_last = (((1,), (1,)), ((), ()))

    def score(slot, k):
        part = proj[slot, :, span(k)]
        wide = part.astype(f32)
        halved = (f32(-0.5) * wide * wide).astype(bf16)
        crossed = lax.dot_general(
            weighted[0:count, span(k)], part, contract_last, preferred_element_type=f32
        )
        damping = lax.dot_general(
            ctf_sq[0:count, span(k)], halved, contract_last, preferred_element_type=f32
        )
        scores[slot, 0:count, 0:rows] += crossed + damping

    def score_step(k, carry):
        direct(k).wait_recv()
        relay(k).start()
        score(0, k)
        score(2, k)

        @pl.when(k > 0)
        def _():
            relay(k - 1).wait_recv()
            score(1, k - 1)

        return carry

    lax.fori_loop(0, chunks, score_step, 0)
    relay(chunks - 1).wait_recv()
    score(1, chunks - 1)

    first, past = window[0:1, :], window[1:2, :]

    tops = []
    for slot in range(SPAN):
        turned = jnp.transpose(scores[slot])[0:rows, :]
        index = lax.broadcasted_iota(jnp.int32, (rows, pad_count), 0) // classes
        index = index + slot * (rows // classes)
        masked = jnp.where((index >= first) & (index < past), turned, -jnp.inf)
        logits[slot * rows : (slot + 1) * rows, :] = masked
        tops.append(jnp.max(masked, axis=0, keepdims=True))
    top = functools.reduce(jnp.maximum, tops)
    scaled = jnp.exp(logits[...] - top)
    logits[...] = scaled
    total = jnp.sum(scaled, axis=0, keepdims=True)
    top_send[...] = jnp.zeros_like(top_send)
    top_send[0:1, :] = top
    top_send[1:2, :] = total
    top_copies = [
        send(top_send, top_recv.at[n], top_send_sem.at[n], top_recv_sem.at[n], i, cls)
        for n, cls in enumerate(others)
    ]
    for copy in top_copies:
        copy.start()
    for copy in top_copies:
        copy.wait_recv()
    highest = top
    for n in range(len(others)):
        highest = jnp.maximum(highest, top_recv[n, 0:1, :])
    totals = total * jnp.exp(top - highest)
    for n in range(len(others)):
        totals += top_recv[n, 1:2, :] * jnp.exp(top_recv[n, 0:1, :] - highest)
    evidence_ref[...] = (highest + jnp.log(totals))[:, 0:count]
    post[...] = (logits[...] * (jnp.exp(top - highest) / totals)).astype(bf16)

    def part(k):
        return send(
            near.at[:, span(k)], sib_recv.at[:, span(k)],
            part_send_sem.at[k], part_recv_sem.at[k], sib,
        )

    def far_sum(k):
        return send(
            far_send.at[:, span(k)], far_recv.at[:, span(k)],
            sum_send_sem.at[k], sum_recv_sem.at[k], up2,
        )

    post_copies = [
        send(post.at[pl.ds((n + 1) * rows, rows), :], post_recv.at[n],
             post_send_sem.at[n], post_recv_sem.at[n], img)
        for n, img in enumerate((up1, up2))
    ]
    first_core = (core == 0).astype(f32)

    def sum_step(k, carry):
        @pl.when(k < chunks)
        def _():
            sums = jnp.dot(post[...], weighted[:, span(k)], preferred_element_type=f32)
            near[:, span(k)] = sums[rows : 2 * rows]
            part(k).start()
            own[:, span(k)] = sums[0:rows]
            far[lax.rem(k, 2)] = sums[2 * rows :]

        @pl.when(k > 0)
        def _():
            part(k - 1).wait_recv()
            from_sib = sib_recv[:, span(k - 1)]
            far_send[:, span(k - 1)] = (far[lax.rem(k - 1, 2)] + first_core * from_sib).astype(bf16)
            far_sum(k - 1).start()
            own[:, span(k - 1)] += (1.0 - first_core) * from_sib

        return carry

    lax.fori_loop(0, chunks + 1, sum_step, 0)
    for copy in post_copies:
        copy.start()

    for n, copy in enumerate(d_copies):
        copy.wait_recv()
        d_col[n + 1] = column(d_recv[n, 0:1, :])
    for n, copy in enumerate(post_copies):
        copy.wait_recv()
    for lo in range(0, comp, CHUNK):
        width = min(CHUNK, comp - lo)

        def square(g, carry, lo=lo):
            at = pl.ds(pl.multiple_of(g * GROUP, GROUP), GROUP)
            for n in range(2):
                ctf = ctf_of(d_col[n + 1, at, 0:1], freq[0:1, lo : lo + CHUNK])
                ctf_next[n, at, :] = (ctf * ctf).astype(bf16)
            return carry

        lax.fori_loop(0, groups, square, 0)
        weight = jnp.dot(post[0:rows], ctf_sq[:, lo : lo + CHUNK], preferred_element_type=f32)
        for n in range(2):
            weight += jnp.dot(post_recv[n], ctf_next[n], preferred_element_type=f32)
        weight_ref[:, lo : lo + width] = weight[:, :width]

    for k in range(chunks):
        far_sum(k).wait_recv()
        lo, hi = k * CHUNK, min((k + 1) * CHUNK, real)
        data_ref[:, lo:hi] = own[:, lo:hi] + far_recv[:, lo:hi].astype(f32)

    for k in range(chunks):
        direct(k).wait_send()
        relay(k).wait_send()
        part(k).wait_send()
        far_sum(k).wait_send()
    for copy in d_copies + top_copies + post_copies:
        copy.wait_send()


def body(n_img, cls_n, particles, defocus, freq_sq, projections, priors):
    count, real = particles.shape
    classes, orients, _ = projections.shape
    rows = classes * orients
    comp = real // 2
    chunks = -(-real // CHUNK)
    pad_real = chunks * CHUNK
    pad_count = -(-count // 128) * 128
    f32, bf16 = jnp.float32, jnp.bfloat16
    dma = pltpu.SemaphoreType.DMA
    vmem = pl.BlockSpec(memory_space=pltpu.VMEM)
    hbm = pl.BlockSpec(memory_space=pl.ANY)
    data, weight, evidence = pl.pallas_call(
        functools.partial(kernel, n_img, cls_n, classes),
        out_shape=[
            jax.ShapeDtypeStruct((rows, real), f32),
            jax.ShapeDtypeStruct((rows, comp), f32),
            jax.ShapeDtypeStruct((1, count), f32),
        ],
        in_specs=[hbm, vmem, vmem, hbm, vmem],
        out_specs=[vmem, vmem, vmem],
        scratch_shapes=[
            pltpu.VMEM((SLOTS, GROUP, real), bf16),
            pltpu.VMEM((rows, real), bf16),
            pltpu.VMEM((SPAN, rows, pad_real), bf16),
            pltpu.VMEM((pad_count, pad_real), bf16),
            pltpu.VMEM((pad_count, pad_real), bf16),
            pltpu.VMEM((8, pad_real), f32),
            pltpu.VMEM((8, pad_count), f32),
            pltpu.VMEM((2, 8, pad_count), f32),
            pltpu.VMEM((SPAN, pad_count, 128), f32),
            pltpu.VMEM((SPAN, pad_count, 128), f32),
            pltpu.VMEM((SPAN * rows, pad_count), f32),
            pltpu.VMEM((SPAN * rows, pad_count), bf16),
            pltpu.VMEM((2, rows, pad_count), bf16),
            pltpu.VMEM((8, pad_count), jnp.int32),
            pltpu.VMEM((8, pad_count), f32),
            pltpu.VMEM((3, 8, pad_count), f32),
            pltpu.VMEM((rows, pad_real), f32),
            pltpu.VMEM((rows, pad_real), f32),
            pltpu.VMEM((2, rows, CHUNK), f32),
            pltpu.VMEM((rows, pad_real), bf16),
            pltpu.VMEM((rows, pad_real), f32),
            pltpu.VMEM((rows, pad_real), bf16),
            pltpu.VMEM((2, pad_count, CHUNK), bf16),
            dma((SLOTS,)), dma, dma((2,)), dma((2,)),
            dma((chunks,)), dma((chunks,)), dma((chunks,)), dma((chunks,)),
            dma((3,)), dma((3,)), dma((2,)), dma((2,)),
            dma((chunks,)), dma((chunks,)), dma((chunks,)), dma((chunks,)),
        ],
        compiler_params=pltpu.CompilerParams(
            collective_id=0, has_side_effects=True, vmem_limit_bytes=60 * 2**20
        ),
    )(
        particles,
        defocus.reshape(1, count),
        freq_sq.reshape(1, comp),
        jnp.transpose(projections, (1, 0, 2)).reshape(rows, real),
        priors.T,
    )

    def placed(sums):
        return jnp.transpose(sums.reshape(orients, classes, sums.shape[1]), (1, 0, 2))

    return placed(data), placed(weight), evidence.reshape(count)


def solution(mesh):
    return jax.shard_map(
        functools.partial(body, mesh.shape["img"], mesh.shape["cls"]),
        mesh=mesh,
        in_specs=(P("img", None), P("img"), P(), P("cls", "img", None), P("img", None)),
        out_specs=(P("cls", "img", None), P("cls", "img", None), P("img")),
        check_vma=False,
    )
```
